32 devices in a mesh: sample: 2 (over y), gx: 8 (over z, x), gy: 2 (over core).
Axes of the slice: x: 2, y: 2, z: 4, core: 2. Of those that a mesh axis runs over, the one named last changes fastest.
Arguments:
- displacement: float32 [2, 128, 1024], P(None, ('sample', 'gx'), 'gy'), parts along dimension 1, may hold values from -5 to 5
- velocity: float32 [2, 128, 1024], P(None, ('sample', 'gx'), 'gy'), parts along dimension 1, may hold values from -5 to 5
- pressure: float32 [128, 1024], P(('sample', 'gx'), 'gy'), parts along dimension 0, may hold values from -5 to 5
- broken_bits: int32 [10, 128, 1024], P(None, ('sample', 'gx'), 'gy'), parts along dimension 1, may hold values from 0 to 4095
- material_class: int32 [128, 1024], P(('sample', 'gx'), 'gy'), parts along dimension 0, may hold values from 0 to 3
- property_table: float32 [8, 4], P('sample'), parts along dimension 0, may hold values from 0.5 to 2
Outputs:
- final_displacement: float32 [2, 128, 1024], P(None, ('sample', 'gx'), 'gy'), parts along dimension 1
- final_velocity: float32 [2, 128, 1024], P(None, ('sample', 'gx'), 'gy'), parts along dimension 1
- final_pressure: float32 [128, 1024], P(('sample', 'gx'), 'gy'), parts along dimension 0
The draws below stay inside these ranges and needn't reach their ends.
There are 2 independent parts, one for each index of `sample`. The reference program is written for one: setup_inputs(seed, part) draws one part's arguments, and reference() takes and returns one part's arrays. A program takes and returns all parts, laid end to end along the dimension named above; each array names one. Nothing has to cross between parts.
Inputs may be any that keep to these rules, and one draw needn't show every extreme that they name: `broken_bits`: bits 12 and above of each word are 0.
All inputs are finite; a program needn't handle non-finite values.
Results may differ from the reference program's by a relative error of at most 0.00002.
Values sent between devices are 32-bit elements; how exact they have to be, the bound alone decides.
A program may use at most 64 MiB of HBM per device.

```python
import math
import jax
import jax.numpy as jnp

STEPS = 2
WORDS = 10
CLASSES = 4
NX = 64
NY = 1024


def touch_ends(array, rng, least, top_value):
    longest = array.shape.index(max(array.shape))
    spots = []
    for shift in (0, 1):
        where = [jax.random.randint(jax.random.fold_in(rng, axis), (), 0, length) for axis, length in enumerate(array.shape)]
        where[longest] = (where[longest] + shift) % array.shape[longest]
        spots.append(tuple(where))
    return array.at[spots[0]].set(least).at[spots[1]].set(top_value)


def block_scale(stream_key, dims, pieces, low, top_value):
    def one(dim, parts):
        heights = jax.random.uniform(jax.random.fold_in(jax.random.fold_in(stream_key, 6), dim), (parts,), jnp.float32, low / len(pieces), top_value / len(pieces))
        return jnp.repeat(jnp.exp(heights), dims[dim] // parts).reshape((-1,) + (1,) * (len(dims) - dim - 1))

    loudness = one(*pieces[0])
    for cut in pieces[1:]:
        loudness = loudness * one(*cut)
    return loudness


def noise(rng, extent, scale, reach, pieces=(), dtype=jnp.bfloat16):
    level = block_scale(rng, extent, pieces, -0.22, 0.18) if pieces else 1.0
    entries = jax.random.normal(rng, extent, jnp.float32) * scale * level
    return jnp.minimum(jnp.maximum(entries, -reach), reach).astype(dtype)


def setup_inputs(seed: int = 0, part: int = 0) -> dict:
    key_of = jax.random.split(jax.random.key(seed), 7)
    part_keys = jax.random.split(jax.random.fold_in(key_of[6], part), 7)
    return {
        "displacement": noise(part_keys[0], (2, NX, NY), 1.0, 5.0, ((1, 8), (2, 2)), jnp.float32),
        "velocity": noise(part_keys[1], (2, NX, NY), 1.0, 5.0, ((1, 8), (2, 2)), jnp.float32),
        "pressure": noise(part_keys[2], (NX, NY), 1.0, 5.0, ((0, 8), (1, 2)), jnp.float32),
        "broken_bits": touch_ends(jax.random.randint(part_keys[3], (WORDS, NX, NY), 0, 4096), jax.random.fold_in(part_keys[3], 1), 0, 4095).astype(jnp.int32),
        "material_class": touch_ends(jax.random.randint(part_keys[4], (NX, NY), 0, CLASSES), jax.random.fold_in(part_keys[4], 1), 0, CLASSES - 1).astype(jnp.int32),
        "property_table": jnp.clip(jnp.exp(jax.random.uniform(part_keys[5], (CLASSES, 4), jnp.float32, math.log(0.5), math.log(2.0))), 0.5, 2.0),
    }


bond_offsets = [(row_step, col_step) for row_step in range(-6, 7) for col_step in range(-6, 7) if 0 < row_step * row_step + col_step * col_step <= 37]

def material_of(material_class, property_table):
    material = jnp.zeros((4,) + material_class.shape, jnp.float32)
    for klass in range(property_table.shape[0]):
        chosen = jnp.where(material_class == klass, 1.0, 0.0).astype(jnp.float32)
        material = material + chosen[None] * property_table[klass][:, None, None]
    return material

def advance(padded, fields, padded_material, material, broken_bits, velocity):
    height, breadth = (fields.shape[1], fields.shape[2])
    force_x = jnp.zeros((height, breadth), jnp.float32)
    force_y = jnp.zeros((height, breadth), jnp.float32)
    dilation = jnp.zeros((height, breadth), jnp.float32)
    inflow = jnp.zeros((height, breadth), jnp.float32)
    for bond_index, (row_step, col_step) in enumerate(bond_offsets):
        beyond = padded[:, 6 + row_step:6 + row_step + height, 6 + col_step:6 + col_step + breadth]
        other = padded_material[:, 6 + row_step:6 + row_step + height, 6 + col_step:6 + col_step + breadth]
        length = math.sqrt(row_step * row_step + col_step * col_step)
        word = broken_bits[bond_index // 12]
        intact = (1 - jnp.bitwise_and(jnp.right_shift(word, bond_index % 12), 1)).astype(jnp.float32)
        stretch = (row_step * (beyond[0] - fields[0]) + col_step * (beyond[1] - fields[1])) / (length * length)
        bond_stiff = 2.0 * material[0] * other[0] / (material[0] + other[0])
        bond_perm = 2.0 * material[1] * other[1] / (material[1] + other[1])
        magnitude = intact * bond_stiff * (stretch - 0.5 * (fields[2] + beyond[2]) * 0.5) / length
        force_x = force_x + magnitude * (row_step / length)
        force_y = force_y + magnitude * (col_step / length)
        dilation = dilation + intact * bond_stiff * stretch / length
        inflow = inflow + intact * bond_perm * (beyond[2] - fields[2]) / (length * length)
    force = jnp.stack([force_x, force_y])
    new_velocity = velocity + 0.1 * (material[2][None] * force - 0.5 * velocity)
    new_displacement = fields[:2] + 0.1 * new_velocity
    new_pressure = fields[2] + 0.1 * material[3] * 0.1 * (inflow - dilation)
    return (new_displacement, new_velocity, new_pressure)

def reference(displacement, velocity, pressure, broken_bits, material_class, property_table):
    material = material_of(material_class, property_table)
    padded_material = jnp.pad(material, ((0, 0), (6, 6), (6, 6)))
    for iteration in range(STEPS):
        fields = jnp.concatenate([displacement, pressure[None]], axis=0)
        padded = jnp.pad(fields, ((0, 0), (6, 6), (6, 6)))
        displacement, velocity, pressure = advance(padded, fields, padded_material, material, broken_bits, velocity)
    return (displacement, velocity, pressure)
```

```python
import functools
import math

import jax
import jax.numpy as jnp
from jax import lax
from jax.experimental import pallas as pl
from jax.experimental.pallas import tpu as pltpu
from jax.sharding import PartitionSpec as P

REACH = 6
MESH = pl.DeviceIdType.MESH
LANES = 128
FAR = 3.0e38

half_width = {a: math.isqrt(37 - a * a) for a in range(-REACH, REACH + 1)}
first_bond = {}
_count = 0
for _a in range(-REACH, REACH + 1):
    first_bond[_a] = _count
    _count += 2 * half_width[_a] + 1 - (1 if _a == 0 else 0)
BONDS = _count

groups = (
    ((-1, 0, 1), (-6, -5, -4, -3, -2, -1, 1, 2, 3, 4, 5, 6)),
    ((-3, -2, 2, 3), tuple(range(-5, 6))),
    ((-4, 4), tuple(range(-4, 5))),
    ((-5, 5), tuple(range(-3, 4))),
    ((-6, 6), tuple(range(-1, 2))),
    ((-1, 1), (0,)),
)


def pick(index, values):
    if isinstance(index, int) or len(set(values)) == 1:
        return values[index if isinstance(index, int) else 0]
    kind = jnp.int32 if isinstance(values[0], int) else jnp.float32
    result = kind(values[-1])
    for i in range(len(values) - 2, -1, -1):
        result = jnp.where(index <= i, kind(values[i]), result)
    return result


def f32(values):
    return [float(v) for v in values]


def over_bonds(carry, visit):
    for cols, rows in groups:

        def body(i, carry, cols=cols, rows=rows):
            b = pick(i, list(cols))
            for a in rows:
                k = first_bond[a] + b + half_width[a]
                if a == 0:
                    k = k - pick(i, [1 if c > 0 else 0 for c in cols])
                carry = visit(carry, i, a, cols, b + REACH, k)
            return carry

        carry = lax.fori_loop(0, len(cols), body, carry)
    return carry


def kernel(
    gx_count, disp, vel, pres, bits, klass, table,
    out_disp, out_vel, out_pres,
    x1, x2, kl, inv, shifted, shifted_inv, wc, wk, bits_v, vel_v,
    local_sem, send_sem, recv_sem, send2_sem, recv2_sem,
):
    sample, gx, gy = lax.axis_index("sample"), lax.axis_index("gx"), lax.axis_index("gy")
    height, breadth = pres.shape
    wide = breadth + LANES
    own = pl.ds(height, height)
    up_rows, down_rows = pl.ds(0, height), pl.ds(2 * height, height)
    cols, side = pl.ds(0, breadth), pl.ds(breadth, LANES)
    edge = pl.ds(pl.multiple_of((1 - gy) * (breadth - LANES), LANES), LANES)
    has_up, has_down = gx > 0, gx < gx_count - 1
    up, down, mate = gx - 1, gx + 1, 1 - gy

    local = [
        pltpu.make_async_copy(klass, kl.at[own, cols], local_sem.at[0]),
        pltpu.make_async_copy(disp, x1.at[pl.ds(0, 2), own, cols], local_sem.at[1]),
        pltpu.make_async_copy(pres, x1.at[2, own, cols], local_sem.at[2]),
        pltpu.make_async_copy(bits, bits_v, local_sem.at[3]),
        pltpu.make_async_copy(vel, vel_v, local_sem.at[4]),
    ]
    for copy in local:
        copy.start()

    barrier = pltpu.get_barrier_semaphore()

    def greet(x, y):
        pl.semaphore_signal(barrier, inc=1, device_id=(sample, x, y), device_id_type=MESH)

    greet(gx, mate)

    @pl.when(has_up)
    def _():
        greet(up, gy)
        greet(up, mate)

    @pl.when(has_down)
    def _():
        greet(down, gy)
        greet(down, mate)

    @pl.when(jnp.logical_not(has_up))
    def _():
        for ref in (x1, x2):
            ref[:, 0:height, :] = jnp.zeros((3, height, wide), jnp.float32)
        kl[0:height, :] = jnp.zeros((height, wide), jnp.int32)

    @pl.when(jnp.logical_not(has_down))
    def _():
        for ref in (x1, x2):
            ref[:, 2 * height : 3 * height, :] = jnp.zeros((3, height, wide), jnp.float32)
        kl[2 * height : 3 * height, :] = jnp.zeros((height, wide), jnp.int32)

    pl.semaphore_wait(
        barrier, 1 + 2 * has_up.astype(jnp.int32) + 2 * has_down.astype(jnp.int32)
    )

    routes = (
        (has_up, has_down, (sample, up, gy), down_rows, True),
        (has_down, has_up, (sample, down, gy), up_rows, True),
        (None, None, (sample, gx, mate), own, False),
        (has_up, has_down, (sample, up, mate), down_rows, False),
        (has_down, has_up, (sample, down, mate), up_rows, False),
    )

    def when(condition, act):
        if condition is None:
            act()
        else:
            pl.when(condition)(act)

    def remote(n, source, target, sends, recvs):
        return pltpu.make_async_remote_copy(
            src_ref=source, dst_ref=target, send_sem=sends.at[n], recv_sem=recvs.at[n],
            device_id=routes[n % 5][2], device_id_type=MESH,
        )

    first = []
    for which in range(3):
        for n, (_, _, _, there, whole) in enumerate(routes):
            here, land = (cols, cols) if whole else (edge, side)
            if which == 0:
                source, target = klass.at[:, here], kl.at[there, land]
            elif which == 1:
                source, target = disp.at[:, :, here], x1.at[pl.ds(0, 2), there, land]
            else:
                source, target = pres.at[:, here], x1.at[2, there, land]
            first.append(remote(which * 5 + n, source, target, send_sem, recv_sem))
    for i, copy in enumerate(first):
        when(routes[i % 5][0], copy.start)

    for i in range(5):
        when(routes[i][1], first[i].wait_recv)
    local[0].wait()
    local[3].wait()

    row = lax.broadcasted_iota(jnp.int32, (3 * height, wide), 0)
    col = lax.broadcasted_iota(jnp.int32, (3 * height, wide), 1)
    low, high = jnp.where(has_up, 0, height), jnp.where(has_down, 3 * height, 2 * height)
    middle = breadth + LANES // 2
    left_side = jnp.where(gy == 0, breadth, middle)
    right_side = jnp.where(gy == 0, middle, wide)
    inside = (row >= low) & (row < high) & (
        (col < breadth) | ((col >= left_side) & (col < right_side))
    )
    classes = table.shape[0]

    def look_up(which, member):
        value = jnp.full(which.shape, table[classes - 1, member], jnp.float32)
        for c in range(classes - 1):
            value = jnp.where(which == c, table[c, member], value)
        return value

    which = kl[...]
    for m in range(2):
        inv[m] = jnp.where(inside, 1.0 / look_up(which, m), FAR)

    def shift_all(source, planes, target):
        for plane in range(planes):
            for t in range(3):
                rows = pl.ds(t * height, height)
                value = source[plane, rows, :]
                for b in range(-REACH, REACH + 1):
                    moved = value if b == 0 else pltpu.roll(value, (-b) % wide, 1)
                    target[b + REACH, plane, rows, :] = moved[:, :breadth]

    shift_all(inv, 2, shifted_inv)
    ic, ik = inv[0, height : 2 * height, :breadth], inv[1, height : 2 * height, :breadth]

    def weigh(carry, i, a, steps, shift, k):
        rows = pl.ds(height + a, height)
        intact = (bits_v[k // 12] & lax.shift_left(jnp.int32(1), k % 12)) == 0
        for here, plane, target in ((ic, 0, wc), (ik, 1, wk)):
            total = here + shifted_inv[shift, plane, rows, :]
            guess = pl.reciprocal(total, approx=True)
            exact = guess * (2.0 - total * guess)
            target[k] = jnp.where(intact, exact, 0.0)
        return carry

    over_bonds(0, weigh)

    for i in range(5, 15):
        when(routes[i % 5][1], first[i].wait_recv)
    for i in (1, 2, 4):
        local[i].wait()

    own_class = kl[height : 2 * height, :breadth]
    density = look_up(own_class, 2)
    storage = look_up(own_class, 3)

    def advance(x, velocity):
        u0, u1, p = (x[f, height : 2 * height, :breadth] for f in range(3))
        shift_all(x, 3, shifted)

        def visit(carry, i, a, steps, shift, k):
            force_x, force_y, dilation, inflow = carry
            rows = pl.ds(height + a, height)
            squares = [a * a + b * b for b in steps]
            q = shifted[shift, 2, rows, :]
            scaled_y = pick(i, f32(2.0 * b / s**2 for b, s in zip(steps, squares)))
            part = scaled_y * (shifted[shift, 1, rows, :] - u1)
            if a != 0:
                scaled_x = pick(i, f32(2.0 * a / s**2 for s in squares))
                part = part + scaled_x * (shifted[shift, 0, rows, :] - u0)
            weight = wc[k]
            pull = weight * part
            mag = pull - weight * (pick(i, f32(0.5 / s for s in squares)) * (q + p))
            if a != 0:
                force_x = force_x + float(a) * mag
            force_y = force_y + pick(i, f32(steps)) * mag
            dilation = dilation + pick(i, f32(math.sqrt(s) for s in squares)) * pull
            inflow = inflow + wk[k] * (pick(i, f32(2.0 / s for s in squares)) * (q - p))
            return force_x, force_y, dilation, inflow

        zero = jnp.zeros((height, breadth), jnp.float32)
        force_x, force_y, dilation, inflow = over_bonds((zero,) * 4, visit)
        v0 = velocity[0] + 0.1 * (density * force_x - 0.5 * velocity[0])
        v1 = velocity[1] + 0.1 * (density * force_y - 0.5 * velocity[1])
        return (
            u0 + 0.1 * v0, u1 + 0.1 * v1, p + 0.1 * storage * 0.1 * (inflow - dilation), v0, v1
        )

    n0, n1, np_, v0, v1 = advance(x1, (vel_v[0], vel_v[1]))
    x2[0, height : 2 * height, :breadth] = n0
    x2[1, height : 2 * height, :breadth] = n1
    x2[2, height : 2 * height, :breadth] = np_
    vel_v[0] = v0
    vel_v[1] = v1

    second = []
    for n, (_, _, _, there, whole) in enumerate(routes):
        here, land = (cols, cols) if whole else (edge, side)
        second.append(
            remote(n, x2.at[:, own, here], x2.at[:, there, land], send2_sem, recv2_sem)
        )
    for i, copy in enumerate(second):
        when(routes[i][0], copy.start)
    for i, copy in enumerate(second):
        when(routes[i][1], copy.wait_recv)

    n0, n1, np_, v0, v1 = advance(x2, (vel_v[0], vel_v[1]))
    out_disp[0] = n0
    out_disp[1] = n1
    out_vel[0] = v0
    out_vel[1] = v1
    out_pres[...] = np_

    for i, copy in enumerate(first):
        when(routes[i % 5][0], copy.wait_send)
    for i, copy in enumerate(second):
        when(routes[i][0], copy.wait_send)


def body(gx_count, displacement, velocity, pressure, broken_bits, material_class, table):
    height, breadth = pressure.shape
    wide = breadth + LANES
    vmem = pl.BlockSpec(memory_space=pltpu.VMEM)
    anywhere = pl.BlockSpec(memory_space=pltpu.HBM)
    smem = pl.BlockSpec(memory_space=pltpu.SMEM)
    f = jnp.float32
    dma = pltpu.SemaphoreType.DMA
    span = 2 * REACH + 1
    return pl.pallas_call(
        functools.partial(kernel, gx_count),
        out_shape=(
            jax.ShapeDtypeStruct((2, height, breadth), f),
            jax.ShapeDtypeStruct((2, height, breadth), f),
            jax.ShapeDtypeStruct((height, breadth), f),
        ),
        in_specs=[anywhere] * 5 + [smem],
        out_specs=(vmem, vmem, vmem),
        scratch_shapes=[
            pltpu.VMEM((3, 3 * height, wide), f),
            pltpu.VMEM((3, 3 * height, wide), f),
            pltpu.VMEM((3 * height, wide), jnp.int32),
            pltpu.VMEM((2, 3 * height, wide), f),
            pltpu.VMEM((span, 3, 3 * height, breadth), f),
            pltpu.VMEM((span, 2, 3 * height, breadth), f),
            pltpu.VMEM((BONDS, height, breadth), f),
            pltpu.VMEM((BONDS, height, breadth), f),
            pltpu.VMEM(broken_bits.shape, jnp.int32),
            pltpu.VMEM((2, height, breadth), f),
            dma((5,)), dma((15,)), dma((15,)), dma((5,)), dma((5,)),
        ],
        compiler_params=pltpu.CompilerParams(
            collective_id=0, has_side_effects=True, vmem_limit_bytes=32 * 1024 * 1024
        ),
        name="peridynamics",
    )(displacement, velocity, pressure, broken_bits, material_class, table)


def solution(mesh):
    plane = P(("sample", "gx"), "gy")
    stack = P(None, ("sample", "gx"), "gy")
    assert mesh.shape["gy"] == 2
    return jax.shard_map(
        functools.partial(body, mesh.shape["gx"]),
        mesh=mesh,
        in_specs=(stack, stack, plane, stack, plane, P("sample", None)),
        out_specs=(stack, stack, plane),
        check_vma=False,
    )
```

```python
import functools
import math

import jax
import jax.numpy as jnp
from jax import lax
from jax.experimental import pallas as pl
from jax.experimental.pallas import tpu as pltpu
from jax.sharding import PartitionSpec as P

REACH = 6
MESH = pl.DeviceIdType.MESH
LANES = 128
FAR = 3.0e38

half_width = {a: math.isqrt(37 - a * a) for a in range(-REACH, REACH + 1)}
first_bond = {}
_count = 0
for _a in range(-REACH, REACH + 1):
    first_bond[_a] = _count
    _count += 2 * half_width[_a] + 1 - (1 if _a == 0 else 0)
BONDS = _count

groups = (
    ((-1, 0, 1), (-6, -5, -4, -3, -2, -1, 1, 2, 3, 4, 5, 6)),
    ((-3, -2, 2, 3), tuple(range(-5, 6))),
    ((-4, 4), tuple(range(-4, 5))),
    ((-5, 5), tuple(range(-3, 4))),
    ((-6, 6), tuple(range(-1, 2))),
    ((-1, 1), (0,)),
)


def pick(index, values):
    if isinstance(index, int) or len(set(values)) == 1:
        return values[index if isinstance(index, int) else 0]
    kind = jnp.int32 if isinstance(values[0], int) else jnp.float32
    result = kind(values[-1])
    for i in range(len(values) - 2, -1, -1):
        result = jnp.where(index <= i, kind(values[i]), result)
    return result


def f32(values):
    return [float(v) for v in values]


def over_bonds(carry, visit):
    for cols, rows in groups:

        def body(i, carry, cols=cols, rows=rows):
            b = pick(i, list(cols))
            for a in rows:
                k = first_bond[a] + b + half_width[a]
                if a == 0:
                    k = k - pick(i, [1 if c > 0 else 0 for c in cols])
                carry = visit(carry, i, a, cols, b + REACH, k)
            return carry

        carry = lax.fori_loop(0, len(cols), body, carry)
    return carry


def kernel(
    gx_count, disp, vel, pres, bits, klass, table,
    out_disp, out_vel, out_pres,
    x1, x2, kl, inv, shifted, shifted_inv, wc, wk, bits_v, vel_v,
    local_sem, send_sem, recv_sem, send2_sem, recv2_sem,
):
    sample, gx, gy = lax.axis_index("sample"), lax.axis_index("gx"), lax.axis_index("gy")
    height, breadth = pres.shape
    wide = breadth + LANES
    own = pl.ds(height, height)
    up_rows, down_rows = pl.ds(0, height), pl.ds(2 * height, height)
    cols, side = pl.ds(0, breadth), pl.ds(breadth, LANES)
    edge = pl.ds(pl.multiple_of((1 - gy) * (breadth - LANES), LANES), LANES)
    has_up, has_down = gx > 0, gx < gx_count - 1
    up, down, mate = gx - 1, gx + 1, 1 - gy

    local = [
        pltpu.make_async_copy(klass, kl.at[own, cols], local_sem.at[0]),
        pltpu.make_async_copy(disp, x1.at[pl.ds(0, 2), own, cols], local_sem.at[1]),
        pltpu.make_async_copy(pres, x1.at[2, own, cols], local_sem.at[2]),
        pltpu.make_async_copy(bits, bits_v, local_sem.at[3]),
        pltpu.make_async_copy(vel, vel_v, local_sem.at[4]),
    ]
    for copy in local:
        copy.start()

    barrier = pltpu.get_barrier_semaphore()

    def greet(x, y):
        pl.semaphore_signal(barrier, inc=1, device_id=(sample, x, y), device_id_type=MESH)

    greet(gx, mate)

    @pl.when(has_up)
    def _():
        greet(up, gy)
        greet(up, mate)

    @pl.when(has_down)
    def _():
        greet(down, gy)
        greet(down, mate)

    @pl.when(jnp.logical_not(has_up))
    def _():
        for ref in (x1, x2):
            ref[:, 0:height, :] = jnp.zeros((3, height, wide), jnp.float32)
        kl[0:height, :] = jnp.zeros((height, wide), jnp.int32)

    @pl.when(jnp.logical_not(has_down))
    def _():
        for ref in (x1, x2):
            ref[:, 2 * height : 3 * height, :] = jnp.zeros((3, height, wide), jnp.float32)
        kl[2 * height : 3 * height, :] = jnp.zeros((height, wide), jnp.int32)

    pl.semaphore_wait(
        barrier, 1 + 2 * has_up.astype(jnp.int32) + 2 * has_down.astype(jnp.int32)
    )

    routes = (
        (has_up, has_down, (sample, up, gy), down_rows, True),
        (has_down, has_up, (sample, down, gy), up_rows, True),
        (None, None, (sample, gx, mate), own, False),
        (has_up, has_down, (sample, up, mate), down_rows, False),
        (has_down, has_up, (sample, down, mate), up_rows, False),
    )

    def when(condition, act):
        if condition is None:
            act()
        else:
            pl.when(condition)(act)

    def remote(n, source, target, sends, recvs):
        return pltpu.make_async_remote_copy(
            src_ref=source, dst_ref=target, send_sem=sends.at[n], recv_sem=recvs.at[n],
            device_id=routes[n % 5][2], device_id_type=MESH,
        )

    first = []
    for which in range(3):
        for n, (_, _, _, there, whole) in enumerate(routes):
            here, land = (cols, cols) if whole else (edge, side)
            if which == 0:
                source, target = klass.at[:, here], kl.at[there, land]
            elif which == 1:
                source, target = disp.at[:, :, here], x1.at[pl.ds(0, 2), there, land]
            else:
                source, target = pres.at[:, here], x1.at[2, there, land]
            first.append(remote(which * 5 + n, source, target, send_sem, recv_sem))
    for i, copy in enumerate(first):
        when(routes[i % 5][0], copy.start)

    for i in range(5):
        when(routes[i][1], first[i].wait_recv)
    local[0].wait()
    local[3].wait()

    row = lax.broadcasted_iota(jnp.int32, (3 * height, wide), 0)
    col = lax.broadcasted_iota(jnp.int32, (3 * height, wide), 1)
    low, high = jnp.where(has_up, 0, height), jnp.where(has_down, 3 * height, 2 * height)
    middle = breadth + LANES // 2
    left_side = jnp.where(gy == 0, breadth, middle)
    right_side = jnp.where(gy == 0, middle, wide)
    inside = (row >= low) & (row < high) & (
        (col < breadth) | ((col >= left_side) & (col < right_side))
    )
    classes = table.shape[0]

    def look_up(which, member):
        value = jnp.full(which.shape, table[classes - 1, member], jnp.float32)
        for c in range(classes - 1):
            value = jnp.where(which == c, table[c, member], value)
        return value

    which = kl[...]
    for m in range(2):
        inv[m] = jnp.where(inside, 1.0 / look_up(which, m), FAR)

    def shift_all(source, planes, target):
        for plane in range(planes):
            for t in range(3):
                rows = pl.ds(t * height, height)
                value = source[plane, rows, :]
                for b in range(-REACH, REACH + 1):
                    moved = value if b == 0 else pltpu.roll(value, (-b) % wide, 1)
                    target[b + REACH, plane, rows, :] = moved[:, :breadth]

    shift_all(inv, 2, shifted_inv)
    ic, ik = inv[0, height : 2 * height, :breadth], inv[1, height : 2 * height, :breadth]

    def weigh(carry, i, a, steps, shift, k):
        rows = pl.ds(height + a, height)
        intact = (bits_v[k // 12] & lax.shift_left(jnp.int32(1), k % 12)) == 0
        for here, plane, target in ((ic, 0, wc), (ik, 1, wk)):
            total = here + shifted_inv[shift, plane, rows, :]
            guess = pl.reciprocal(total, approx=True)
            exact = guess * (2.0 - total * guess)
            target[k] = jnp.where(intact, exact, 0.0)
        return carry

    over_bonds(0, weigh)

    for i in range(5, 15):
        when(routes[i % 5][1], first[i].wait_recv)
    for i in (1, 2, 4):
        local[i].wait()

    own_class = kl[height : 2 * height, :breadth]
    density = look_up(own_class, 2)
    storage = look_up(own_class, 3)

    def advance(x, velocity):
        u0, u1, p = (x[f, height : 2 * height, :breadth] for f in range(3))
        shift_all(x, 3, shifted)

        def visit(carry, i, a, steps, shift, k):
            force_x, force_y, dilation, inflow = carry
            rows = pl.ds(height + a, height)
            squares = [a * a + b * b for b in steps]
            q = shifted[shift, 2, rows, :]
            scaled_y = pick(i, f32(2.0 * b / s**2 for b, s in zip(steps, squares)))
            part = scaled_y * (shifted[shift, 1, rows, :] - u1)
            if a != 0:
                scaled_x = pick(i, f32(2.0 * a / s**2 for s in squares))
                part = part + scaled_x * (shifted[shift, 0, rows, :] - u0)
            weight = wc[k]
            pull = weight * part
            mag = pull - weight * (pick(i, f32(0.5 / s for s in squares)) * (q + p))
            if a != 0:
                force_x = force_x + float(a) * mag
            force_y = force_y + pick(i, f32(steps)) * mag
            dilation = dilation + pick(i, f32(math.sqrt(s) for s in squares)) * pull
            inflow = inflow + wk[k] * (pick(i, f32(2.0 / s for s in squares)) * (q - p))
            return force_x, force_y, dilation, inflow

        zero = jnp.zeros((height, breadth), jnp.float32)
        force_x, force_y, dilation, inflow = over_bonds((zero,) * 4, visit)
        v0 = velocity[0] + 0.1 * (density * force_x - 0.5 * velocity[0])
        v1 = velocity[1] + 0.1 * (density * force_y - 0.5 * velocity[1])
        return (
            u0 + 0.1 * v0, u1 + 0.1 * v1, p + 0.1 * storage * 0.1 * (inflow - dilation), v0, v1
        )

    n0, n1, np_, v0, v1 = advance(x1, (vel_v[0], vel_v[1]))
    x2[0, height : 2 * height, :breadth] = n0
    x2[1, height : 2 * height, :breadth] = n1
    x2[2, height : 2 * height, :breadth] = np_
    vel_v[0] = v0
    vel_v[1] = v1

    second = []
    for n, (_, _, _, there, whole) in enumerate(routes):
        here, land = (cols, cols) if whole else (edge, side)
        second.append(
            remote(n, x2.at[:, own, here], x2.at[:, there, land], send2_sem, recv2_sem)
        )
    for i, copy in enumerate(second):
        when(routes[i][0], copy.start)
    for i, copy in enumerate(second):
        when(routes[i][1], copy.wait_recv)

    n0, n1, np_, v0, v1 = advance(x2, (vel_v[0], vel_v[1]))
    out_disp[0] = n0
    out_disp[1] = n1
    out_vel[0] = v0
    out_vel[1] = v1
    out_pres[...] = np_

    for i, copy in enumerate(first):
        when(routes[i % 5][0], copy.wait_send)
    for i, copy in enumerate(second):
        when(routes[i][0], copy.wait_send)


def body(gx_count, displacement, velocity, pressure, broken_bits, material_class, table):
    height, breadth = pressure.shape
    wide = breadth + LANES
    vmem = pl.BlockSpec(memory_space=pltpu.VMEM)
    anywhere = pl.BlockSpec(memory_space=pltpu.HBM)
    smem = pl.BlockSpec(memory_space=pltpu.SMEM)
    f = jnp.float32
    dma = pltpu.SemaphoreType.DMA
    span = 2 * REACH + 1
    return pl.pallas_call(
        functools.partial(kernel, gx_count),
        out_shape=(
            jax.ShapeDtypeStruct((2, height, breadth), f),
            jax.ShapeDtypeStruct((2, height, breadth), f),
            jax.ShapeDtypeStruct((height, breadth), f),
        ),
        in_specs=[anywhere] * 5 + [smem],
        out_specs=(vmem, vmem, vmem),
        scratch_shapes=[
            pltpu.VMEM((3, 3 * height, wide), f),
            pltpu.VMEM((3, 3 * height, wide), f),
            pltpu.VMEM((3 * height, wide), jnp.int32),
            pltpu.VMEM((2, 3 * height, wide), f),
            pltpu.VMEM((span, 3, 3 * height, breadth), f),
            pltpu.VMEM((span, 2, 3 * height, breadth), f),
            pltpu.VMEM((BONDS, height, breadth), f),
            pltpu.VMEM((BONDS, height, breadth), f),
            pltpu.VMEM(broken_bits.shape, jnp.int32),
            pltpu.VMEM((2, height, breadth), f),
            dma((5,)), dma((15,)), dma((15,)), dma((5,)), dma((5,)),
        ],
        compiler_params=pltpu.CompilerParams(
            collective_id=0, has_side_effects=True, vmem_limit_bytes=62 * 1024 * 1024
        ),
        name="peridynamics",
    )(displacement, velocity, pressure, broken_bits, material_class, table)


def solution(mesh):
    plane = P(("sample", "gx"), "gy")
    stack = P(None, ("sample", "gx"), "gy")
    assert mesh.shape["gy"] == 2
    return jax.shard_map(
        functools.partial(body, mesh.shape["gx"]),
        mesh=mesh,
        in_specs=(stack, stack, plane, stack, plane, P("sample", None)),
        out_specs=(stack, stack, plane),
        check_vma=False,
    )
```

```python
import functools
import math

import jax
import jax.numpy as jnp
from jax import lax
from jax.experimental import pallas as pl
from jax.experimental.pallas import tpu as pltpu
from jax.sharding import PartitionSpec as P

REACH = 6
MESH = pl.DeviceIdType.MESH
LANES = 128
FAR = 3.0e38

half_width = {a: math.isqrt(37 - a * a) for a in range(-REACH, REACH + 1)}
first_bond = {}
_count = 0
for _a in range(-REACH, REACH + 1):
    first_bond[_a] = _count
    _count += 2 * half_width[_a] + 1 - (1 if _a == 0 else 0)
BONDS = _count

groups = (
    ((-1, 0, 1), (-6, -5, -4, -3, -2, -1, 1, 2, 3, 4, 5, 6)),
    ((-3, -2, 2, 3), tuple(range(-5, 6))),
    ((-4, 4), tuple(range(-4, 5))),
    ((-5, 5), tuple(range(-3, 4))),
    ((-6, 6), tuple(range(-1, 2))),
    ((-1, 1), (0,)),
)


def pick(index, values):
    if isinstance(index, int) or len(set(values)) == 1:
        return values[index if isinstance(index, int) else 0]
    kind = jnp.int32 if isinstance(values[0], int) else jnp.float32
    result = kind(values[-1])
    for i in range(len(values) - 2, -1, -1):
        result = jnp.where(index <= i, kind(values[i]), result)
    return result


def f32(values):
    return [float(v) for v in values]


def over_bonds(carry, visit):
    for cols, rows in groups:

        def body(i, carry, cols=cols, rows=rows):
            b = pick(i, list(cols))
            for a in rows:
                k = first_bond[a] + b + half_width[a]
                if a == 0:
                    k = k - pick(i, [1 if c > 0 else 0 for c in cols])
                carry = visit(carry, i, a, cols, b + REACH, k)
            return carry

        for i in range(len(cols)):
            carry = body(i, carry)
    return carry


def kernel(
    gx_count, disp, vel, pres, bits, klass, table,
    out_disp, out_vel, out_pres,
    x1, x2, kl, inv, shifted, shifted_inv, wc, wk, bits_v, vel_v,
    local_sem, send_sem, recv_sem, send2_sem, recv2_sem,
):
    sample, gx, gy = lax.axis_index("sample"), lax.axis_index("gx"), lax.axis_index("gy")
    height, breadth = pres.shape
    wide = breadth + LANES
    own = pl.ds(height, height)
    up_rows, down_rows = pl.ds(0, height), pl.ds(2 * height, height)
    cols, side = pl.ds(0, breadth), pl.ds(breadth, LANES)
    edge = pl.ds(pl.multiple_of((1 - gy) * (breadth - LANES), LANES), LANES)
    has_up, has_down = gx > 0, gx < gx_count - 1
    up, down, mate = gx - 1, gx + 1, 1 - gy

    local = [
        pltpu.make_async_copy(klass, kl.at[own, cols], local_sem.at[0]),
        pltpu.make_async_copy(disp, x1.at[pl.ds(0, 2), own, cols], local_sem.at[1]),
        pltpu.make_async_copy(pres, x1.at[2, own, cols], local_sem.at[2]),
        pltpu.make_async_copy(bits, bits_v, local_sem.at[3]),
        pltpu.make_async_copy(vel, vel_v, local_sem.at[4]),
    ]
    for copy in local:
        copy.start()

    barrier = pltpu.get_barrier_semaphore()

    def greet(x, y):
        pl.semaphore_signal(barrier, inc=1, device_id=(sample, x, y), device_id_type=MESH)

    greet(gx, mate)

    @pl.when(has_up)
    def _():
        greet(up, gy)
        greet(up, mate)

    @pl.when(has_down)
    def _():
        greet(down, gy)
        greet(down, mate)

    @pl.when(jnp.logical_not(has_up))
    def _():
        for ref in (x1, x2):
            ref[:, 0:height, :] = jnp.zeros((3, height, wide), jnp.float32)
        kl[0:height, :] = jnp.zeros((height, wide), jnp.int32)

    @pl.when(jnp.logical_not(has_down))
    def _():
        for ref in (x1, x2):
            ref[:, 2 * height : 3 * height, :] = jnp.zeros((3, height, wide), jnp.float32)
        kl[2 * height : 3 * height, :] = jnp.zeros((height, wide), jnp.int32)

    pl.semaphore_wait(
        barrier, 1 + 2 * has_up.astype(jnp.int32) + 2 * has_down.astype(jnp.int32)
    )

    routes = (
        (has_up, has_down, (sample, up, gy), down_rows, True),
        (has_down, has_up, (sample, down, gy), up_rows, True),
        (None, None, (sample, gx, mate), own, False),
        (has_up, has_down, (sample, up, mate), down_rows, False),
        (has_down, has_up, (sample, down, mate), up_rows, False),
    )

    def when(condition, act):
        if condition is None:
            act()
        else:
            pl.when(condition)(act)

    def remote(n, source, target, sends, recvs):
        return pltpu.make_async_remote_copy(
            src_ref=source, dst_ref=target, send_sem=sends.at[n], recv_sem=recvs.at[n],
            device_id=routes[n % 5][2], device_id_type=MESH,
        )

    first = []
    for which in range(3):
        for n, (_, _, _, there, whole) in enumerate(routes):
            here, land = (cols, cols) if whole else (edge, side)
            if which == 0:
                source, target = klass.at[:, here], kl.at[there, land]
            elif which == 1:
                source, target = disp.at[:, :, here], x1.at[pl.ds(0, 2), there, land]
            else:
                source, target = pres.at[:, here], x1.at[2, there, land]
            first.append(remote(which * 5 + n, source, target, send_sem, recv_sem))
    for i, copy in enumerate(first):
        when(routes[i % 5][0], copy.start)

    for i in range(5):
        when(routes[i][1], first[i].wait_recv)
    local[0].wait()
    local[3].wait()

    row = lax.broadcasted_iota(jnp.int32, (3 * height, wide), 0)
    col = lax.broadcasted_iota(jnp.int32, (3 * height, wide), 1)
    low, high = jnp.where(has_up, 0, height), jnp.where(has_down, 3 * height, 2 * height)
    middle = breadth + LANES // 2
    left_side = jnp.where(gy == 0, breadth, middle)
    right_side = jnp.where(gy == 0, middle, wide)
    inside = (row >= low) & (row < high) & (
        (col < breadth) | ((col >= left_side) & (col < right_side))
    )
    classes = table.shape[0]

    def look_up(which, member):
        value = jnp.full(which.shape, table[classes - 1, member], jnp.float32)
        for c in range(classes - 1):
            value = jnp.where(which == c, table[c, member], value)
        return value

    which = kl[...]
    for m in range(2):
        inv[m] = jnp.where(inside, 1.0 / look_up(which, m), FAR)

    def shift_all(source, planes, target):
        for plane in range(planes):
            for t in range(3):
                rows = pl.ds(t * height, height)
                value = source[plane, rows, :]
                for b in range(-REACH, REACH + 1):
                    moved = value if b == 0 else pltpu.roll(value, (-b) % wide, 1)
                    target[b + REACH, plane, rows, :] = moved[:, :breadth]

    shift_all(inv, 2, shifted_inv)
    ic, ik = inv[0, height : 2 * height, :breadth], inv[1, height : 2 * height, :breadth]

    def weigh(carry, i, a, steps, shift, k):
        rows = pl.ds(height + a, height)
        intact = (bits_v[k // 12] & lax.shift_left(jnp.int32(1), k % 12)) == 0
        for here, plane, target in ((ic, 0, wc), (ik, 1, wk)):
            total = here + shifted_inv[shift, plane, rows, :]
            guess = pl.reciprocal(total, approx=True)
            exact = guess * (2.0 - total * guess)
            target[k] = jnp.where(intact, exact, 0.0)
        return carry

    over_bonds(0, weigh)

    for i in range(5, 15):
        when(routes[i % 5][1], first[i].wait_recv)
    for i in (1, 2, 4):
        local[i].wait()

    own_class = kl[height : 2 * height, :breadth]
    density = look_up(own_class, 2)
    storage = look_up(own_class, 3)

    def advance(x, velocity):
        u0, u1, p = (x[f, height : 2 * height, :breadth] for f in range(3))
        shift_all(x, 3, shifted)

        def visit(carry, i, a, steps, shift, k):
            force_x, force_y, dilation, inflow = carry
            rows = pl.ds(height + a, height)
            squares = [a * a + b * b for b in steps]
            q = shifted[shift, 2, rows, :]
            scaled_y = pick(i, f32(2.0 * b / s**2 for b, s in zip(steps, squares)))
            part = scaled_y * (shifted[shift, 1, rows, :] - u1)
            if a != 0:
                scaled_x = pick(i, f32(2.0 * a / s**2 for s in squares))
                part = part + scaled_x * (shifted[shift, 0, rows, :] - u0)
            weight = wc[k]
            pull = weight * part
            mag = pull - weight * (pick(i, f32(0.5 / s for s in squares)) * (q + p))
            if a != 0:
                force_x = force_x + float(a) * mag
            force_y = force_y + pick(i, f32(steps)) * mag
            dilation = dilation + pick(i, f32(math.sqrt(s) for s in squares)) * pull
            inflow = inflow + wk[k] * (pick(i, f32(2.0 / s for s in squares)) * (q - p))
            return force_x, force_y, dilation, inflow

        zero = jnp.zeros((height, breadth), jnp.float32)
        force_x, force_y, dilation, inflow = over_bonds((zero,) * 4, visit)
        v0 = velocity[0] + 0.1 * (density * force_x - 0.5 * velocity[0])
        v1 = velocity[1] + 0.1 * (density * force_y - 0.5 * velocity[1])
        return (
            u0 + 0.1 * v0, u1 + 0.1 * v1, p + 0.1 * storage * 0.1 * (inflow - dilation), v0, v1
        )

    n0, n1, np_, v0, v1 = advance(x1, (vel_v[0], vel_v[1]))
    x2[0, height : 2 * height, :breadth] = n0
    x2[1, height : 2 * height, :breadth] = n1
    x2[2, height : 2 * height, :breadth] = np_
    vel_v[0] = v0
    vel_v[1] = v1

    second = []
    for n, (_, _, _, there, whole) in enumerate(routes):
        here, land = (cols, cols) if whole else (edge, side)
        second.append(
            remote(n, x2.at[:, own, here], x2.at[:, there, land], send2_sem, recv2_sem)
        )
    for i, copy in enumerate(second):
        when(routes[i][0], copy.start)
    for i, copy in enumerate(second):
        when(routes[i][1], copy.wait_recv)

    n0, n1, np_, v0, v1 = advance(x2, (vel_v[0], vel_v[1]))
    out_disp[0] = n0
    out_disp[1] = n1
    out_vel[0] = v0
    out_vel[1] = v1
    out_pres[...] = np_

    for i, copy in enumerate(first):
        when(routes[i % 5][0], copy.wait_send)
    for i, copy in enumerate(second):
        when(routes[i][0], copy.wait_send)


def body(gx_count, displacement, velocity, pressure, broken_bits, material_class, table):
    height, breadth = pressure.shape
    wide = breadth + LANES
    vmem = pl.BlockSpec(memory_space=pltpu.VMEM)
    anywhere = pl.BlockSpec(memory_space=pltpu.HBM)
    smem = pl.BlockSpec(memory_space=pltpu.SMEM)
    f = jnp.float32
    dma = pltpu.SemaphoreType.DMA
    span = 2 * REACH + 1
    return pl.pallas_call(
        functools.partial(kernel, gx_count),
        out_shape=(
            jax.ShapeDtypeStruct((2, height, breadth), f),
            jax.ShapeDtypeStruct((2, height, breadth), f),
            jax.ShapeDtypeStruct((height, breadth), f),
        ),
        in_specs=[anywhere] * 5 + [smem],
        out_specs=(vmem, vmem, vmem),
        scratch_shapes=[
            pltpu.VMEM((3, 3 * height, wide), f),
            pltpu.VMEM((3, 3 * height, wide), f),
            pltpu.VMEM((3 * height, wide), jnp.int32),
            pltpu.VMEM((2, 3 * height, wide), f),
            pltpu.VMEM((span, 3, 3 * height, breadth), f),
            pltpu.VMEM((span, 2, 3 * height, breadth), f),
            pltpu.VMEM((BONDS, height, breadth), f),
            pltpu.VMEM((BONDS, height, breadth), f),
            pltpu.VMEM(broken_bits.shape, jnp.int32),
            pltpu.VMEM((2, height, breadth), f),
            dma((5,)), dma((15,)), dma((15,)), dma((5,)), dma((5,)),
        ],
        compiler_params=pltpu.CompilerParams(
            collective_id=0, has_side_effects=True, vmem_limit_bytes=62 * 1024 * 1024
        ),
        name="peridynamics",
    )(displacement, velocity, pressure, broken_bits, material_class, table)


def solution(mesh):
    plane = P(("sample", "gx"), "gy")
    stack = P(None, ("sample", "gx"), "gy")
    assert mesh.shape["gy"] == 2
    return jax.shard_map(
        functools.partial(body, mesh.shape["gx"]),
        mesh=mesh,
        in_specs=(stack, stack, plane, stack, plane, P("sample", None)),
        out_specs=(stack, stack, plane),
        check_vma=False,
    )
```

```python
import functools
import math

import jax
import jax.numpy as jnp
from jax import lax
from jax.experimental import pallas as pl
from jax.experimental.pallas import tpu as pltpu
from jax.sharding import PartitionSpec as P

REACH = 6
MESH = pl.DeviceIdType.MESH
LANES = 128
FAR = 3.0e38

half_width = {a: math.isqrt(37 - a * a) for a in range(-REACH, REACH + 1)}
first_bond = {}
_count = 0
for _a in range(-REACH, REACH + 1):
    first_bond[_a] = _count
    _count += 2 * half_width[_a] + 1 - (1 if _a == 0 else 0)
BONDS = _count

groups = (
    ((-1, 0, 1), (-6, -5, -4, -3, -2, -1, 1, 2, 3, 4, 5, 6)),
    ((-3, -2, 2, 3), tuple(range(-5, 6))),
    ((-4, 4), tuple(range(-4, 5))),
    ((-5, 5), tuple(range(-3, 4))),
    ((-6, 6), tuple(range(-1, 2))),
    ((-1, 1), (0,)),
)


def pick(index, values):
    if isinstance(index, int) or len(set(values)) == 1:
        return values[index if isinstance(index, int) else 0]
    kind = jnp.int32 if isinstance(values[0], int) else jnp.float32
    result = kind(values[-1])
    for i in range(len(values) - 2, -1, -1):
        result = jnp.where(index <= i, kind(values[i]), result)
    return result


def f32(values):
    return [float(v) for v in values]


def over_bonds(carry, visit):
    for cols, rows in groups:

        def body(i, carry, cols=cols, rows=rows):
            b = pick(i, list(cols))
            for a in rows:
                k = first_bond[a] + b + half_width[a]
                if a == 0:
                    k = k - pick(i, [1 if c > 0 else 0 for c in cols])
                carry = visit(carry, i, a, cols, b + REACH, k)
            return carry

        for i in range(len(cols)):
            carry = body(i, carry)
    return carry


def kernel(
    gx_count, disp, vel, pres, bits, klass, table,
    out_disp, out_vel, out_pres,
    x1, x2, kl, inv, shifted, shifted_inv, wc, wk, bits_v, vel_v,
    local_sem, send_sem, recv_sem, send2_sem, recv2_sem,
):
    sample, gx, gy = lax.axis_index("sample"), lax.axis_index("gx"), lax.axis_index("gy")
    height, breadth = pres.shape
    wide = breadth + LANES
    own = pl.ds(height, height)
    up_rows, down_rows = pl.ds(0, height), pl.ds(2 * height, height)
    cols, side = pl.ds(0, breadth), pl.ds(breadth, LANES)
    edge = pl.ds(pl.multiple_of((1 - gy) * (breadth - LANES), LANES), LANES)
    has_up, has_down = gx > 0, gx < gx_count - 1
    up, down, mate = gx - 1, gx + 1, 1 - gy

    local = [
        pltpu.make_async_copy(klass, kl.at[own, cols], local_sem.at[0]),
        pltpu.make_async_copy(disp, x1.at[pl.ds(0, 2), own, cols], local_sem.at[1]),
        pltpu.make_async_copy(pres, x1.at[2, own, cols], local_sem.at[2]),
        pltpu.make_async_copy(bits, bits_v, local_sem.at[3]),
        pltpu.make_async_copy(vel, vel_v, local_sem.at[4]),
    ]
    for copy in local:
        copy.start()

    barrier = pltpu.get_barrier_semaphore()

    def greet(x, y):
        pl.semaphore_signal(barrier, inc=1, device_id=(sample, x, y), device_id_type=MESH)

    greet(gx, mate)

    @pl.when(has_up)
    def _():
        greet(up, gy)
        greet(up, mate)

    @pl.when(has_down)
    def _():
        greet(down, gy)
        greet(down, mate)

    @pl.when(jnp.logical_not(has_up))
    def _():
        for ref in (x1, x2):
            ref[:, 0:height, :] = jnp.zeros((3, height, wide), jnp.float32)
        kl[0:height, :] = jnp.zeros((height, wide), jnp.int32)

    @pl.when(jnp.logical_not(has_down))
    def _():
        for ref in (x1, x2):
            ref[:, 2 * height : 3 * height, :] = jnp.zeros((3, height, wide), jnp.float32)
        kl[2 * height : 3 * height, :] = jnp.zeros((height, wide), jnp.int32)

    pl.semaphore_wait(
        barrier, 1 + 2 * has_up.astype(jnp.int32) + 2 * has_down.astype(jnp.int32)
    )

    routes = (
        (has_up, has_down, (sample, up, gy), down_rows, True),
        (has_down, has_up, (sample, down, gy), up_rows, True),
        (None, None, (sample, gx, mate), own, False),
        (has_up, has_down, (sample, up, mate), down_rows, False),
        (has_down, has_up, (sample, down, mate), up_rows, False),
    )

    def when(condition, act):
        if condition is None:
            act()
        else:
            pl.when(condition)(act)

    def remote(n, source, target, sends, recvs):
        return pltpu.make_async_remote_copy(
            src_ref=source, dst_ref=target, send_sem=sends.at[n], recv_sem=recvs.at[n],
            device_id=routes[n % 5][2], device_id_type=MESH,
        )

    first = []
    for which in range(2):
        for n, (_, _, _, there, whole) in enumerate(routes):
            here, land = (cols, cols) if whole else (edge, side)
            if which == 0:
                source, target = klass.at[:, here], kl.at[there, land]
            else:
                source, target = x1.at[:, own, here], x1.at[:, there, land]
            first.append(remote(which * 5 + n, source, target, send_sem, recv_sem))
    for i, copy in enumerate(first):
        if i == 5:
            local[1].wait()
            local[2].wait()
        when(routes[i % 5][0], copy.start)

    for i in range(5):
        when(routes[i][1], first[i].wait_recv)
    local[0].wait()
    local[3].wait()

    row = lax.broadcasted_iota(jnp.int32, (3 * height, wide), 0)
    col = lax.broadcasted_iota(jnp.int32, (3 * height, wide), 1)
    low, high = jnp.where(has_up, 0, height), jnp.where(has_down, 3 * height, 2 * height)
    middle = breadth + LANES // 2
    left_side = jnp.where(gy == 0, breadth, middle)
    right_side = jnp.where(gy == 0, middle, wide)
    inside = (row >= low) & (row < high) & (
        (col < breadth) | ((col >= left_side) & (col < right_side))
    )
    classes = table.shape[0]

    def look_up(which, member):
        value = jnp.full(which.shape, table[classes - 1, member], jnp.float32)
        for c in range(classes - 1):
            value = jnp.where(which == c, table[c, member], value)
        return value

    which = kl[...]
    for m in range(2):
        inv[m] = jnp.where(inside, 1.0 / look_up(which, m), FAR)

    def shift_all(source, planes, target):
        for plane in range(planes):
            for t in range(3):
                rows = pl.ds(t * height, height)
                value = source[plane, rows, :]
                for b in range(-REACH, REACH + 1):
                    moved = value if b == 0 else pltpu.roll(value, (-b) % wide, 1)
                    target[b + REACH, plane, rows, :] = moved[:, :breadth]

    shift_all(inv, 2, shifted_inv)
    ic, ik = inv[0, height : 2 * height, :breadth], inv[1, height : 2 * height, :breadth]

    def weigh(carry, i, a, steps, shift, k):
        rows = pl.ds(height + a, height)
        intact = (bits_v[k // 12] & lax.shift_left(jnp.int32(1), k % 12)) == 0
        for here, plane, target in ((ic, 0, wc), (ik, 1, wk)):
            total = here + shifted_inv[shift, plane, rows, :]
            guess = pl.reciprocal(total, approx=True)
            exact = guess * (2.0 - total * guess)
            target[k] = jnp.where(intact, exact, 0.0)
        return carry

    over_bonds(0, weigh)

    for i in range(5, 10):
        when(routes[i % 5][1], first[i].wait_recv)
    local[4].wait()

    own_class = kl[height : 2 * height, :breadth]
    density = look_up(own_class, 2)
    storage = look_up(own_class, 3)

    def advance(x, velocity):
        u0, u1, p = (x[f, height : 2 * height, :breadth] for f in range(3))
        shift_all(x, 3, shifted)

        def visit(carry, i, a, steps, shift, k):
            force_x, force_y, dilation, inflow = carry
            rows = pl.ds(height + a, height)
            squares = [a * a + b * b for b in steps]
            q = shifted[shift, 2, rows, :]
            scaled_y = pick(i, f32(2.0 * b / s**2 for b, s in zip(steps, squares)))
            part = scaled_y * (shifted[shift, 1, rows, :] - u1)
            if a != 0:
                scaled_x = pick(i, f32(2.0 * a / s**2 for s in squares))
                part = part + scaled_x * (shifted[shift, 0, rows, :] - u0)
            weight = wc[k]
            pull = weight * part
            mag = pull - weight * (pick(i, f32(0.5 / s for s in squares)) * (q + p))
            if a != 0:
                force_x = force_x + float(a) * mag
            force_y = force_y + pick(i, f32(steps)) * mag
            dilation = dilation + pick(i, f32(math.sqrt(s) for s in squares)) * pull
            inflow = inflow + wk[k] * (pick(i, f32(2.0 / s for s in squares)) * (q - p))
            return force_x, force_y, dilation, inflow

        zero = jnp.zeros((height, breadth), jnp.float32)
        force_x, force_y, dilation, inflow = over_bonds((zero,) * 4, visit)
        v0 = velocity[0] + 0.1 * (density * force_x - 0.5 * velocity[0])
        v1 = velocity[1] + 0.1 * (density * force_y - 0.5 * velocity[1])
        return (
            u0 + 0.1 * v0, u1 + 0.1 * v1, p + 0.1 * storage * 0.1 * (inflow - dilation), v0, v1
        )

    n0, n1, np_, v0, v1 = advance(x1, (vel_v[0], vel_v[1]))
    x2[0, height : 2 * height, :breadth] = n0
    x2[1, height : 2 * height, :breadth] = n1
    x2[2, height : 2 * height, :breadth] = np_
    vel_v[0] = v0
    vel_v[1] = v1

    second = []
    for n, (_, _, _, there, whole) in enumerate(routes):
        here, land = (cols, cols) if whole else (edge, side)
        second.append(
            remote(n, x2.at[:, own, here], x2.at[:, there, land], send2_sem, recv2_sem)
        )
    for i, copy in enumerate(second):
        when(routes[i][0], copy.start)
    for i, copy in enumerate(second):
        when(routes[i][1], copy.wait_recv)

    n0, n1, np_, v0, v1 = advance(x2, (vel_v[0], vel_v[1]))
    out_disp[0] = n0
    out_disp[1] = n1
    out_vel[0] = v0
    out_vel[1] = v1
    out_pres[...] = np_

    for i, copy in enumerate(first):
        when(routes[i % 5][0], copy.wait_send)
    for i, copy in enumerate(second):
        when(routes[i][0], copy.wait_send)


def body(gx_count, displacement, velocity, pressure, broken_bits, material_class, table):
    height, breadth = pressure.shape
    wide = breadth + LANES
    vmem = pl.BlockSpec(memory_space=pltpu.VMEM)
    anywhere = pl.BlockSpec(memory_space=pltpu.HBM)
    smem = pl.BlockSpec(memory_space=pltpu.SMEM)
    f = jnp.float32
    dma = pltpu.SemaphoreType.DMA
    span = 2 * REACH + 1
    return pl.pallas_call(
        functools.partial(kernel, gx_count),
        out_shape=(
            pltpu.VMEM((2, height, breadth), f),
            pltpu.VMEM((2, height, breadth), f),
            pltpu.VMEM((height, breadth), f),
        ),
        in_specs=[anywhere] * 5 + [smem],
        out_specs=(vmem, vmem, vmem),
        scratch_shapes=[
            pltpu.VMEM((3, 3 * height, wide), f),
            pltpu.VMEM((3, 3 * height, wide), f),
            pltpu.VMEM((3 * height, wide), jnp.int32),
            pltpu.VMEM((2, 3 * height, wide), f),
            pltpu.VMEM((span, 3, 3 * height, breadth), f),
            pltpu.VMEM((span, 2, 3 * height, breadth), f),
            pltpu.VMEM((BONDS, height, breadth), f),
            pltpu.VMEM((BONDS, height, breadth), f),
            pltpu.VMEM(broken_bits.shape, jnp.int32),
            pltpu.VMEM((2, height, breadth), f),
            dma((5,)), dma((10,)), dma((10,)), dma((5,)), dma((5,)),
        ],
        compiler_params=pltpu.CompilerParams(
            collective_id=0, has_side_effects=True, vmem_limit_bytes=62 * 1024 * 1024
        ),
        name="peridynamics",
    )(displacement, velocity, pressure, broken_bits, material_class, table)


def solution(mesh):
    plane = P(("sample", "gx"), "gy")
    stack = P(None, ("sample", "gx"), "gy")
    assert mesh.shape["gy"] == 2
    return jax.shard_map(
        functools.partial(body, mesh.shape["gx"]),
        mesh=mesh,
        in_specs=(stack, stack, plane, stack, plane, P("sample", None)),
        out_specs=(stack, stack, plane),
        check_vma=False,
    )
```
